32 devices in a mesh: ctx: 8 (over y, x, core), ch: 4 (over z).
Axes of the slice: x: 2, y: 2, z: 4, core: 2. Of those that a mesh axis runs over, the one named last changes fastest.
Arguments:
- q_proj: bfloat16 [4096, 4096], P(('ctx', 'ch')), may hold values from -6 to 6
- k_proj: bfloat16 [4096, 4096], P(('ctx', 'ch')), may hold values from -6 to 6
- v_proj: bfloat16 [4096, 4096], P(('ctx', 'ch')), may hold values from -6 to 6
- filter_taps: bfloat16 [4096, 4096], P(('ctx', 'ch')), may hold values from -6 to 6
- out_grad: bfloat16 [4096, 4096], P(('ctx', 'ch')), may hold values from -6 to 6
Outputs:
- mixed: bfloat16 [4096, 4096], P(('ctx', 'ch'))
- q_grad: bfloat16 [4096, 4096], P(('ctx', 'ch'))
- k_grad: bfloat16 [4096, 4096], P(('ctx', 'ch'))
- v_grad: bfloat16 [4096, 4096], P(('ctx', 'ch'))
- filter_grad: bfloat16 [4096, 4096], P(('ctx', 'ch'))
The draws below stay inside these ranges and needn't reach their ends.
All inputs are finite; a program needn't handle non-finite values.
Results may differ from the reference program's by a relative error of at most 0.013.
Values may be sent and summed in bfloat16 or wider, within the bound.
A program may use at most 192 MiB of HBM per device.

```python
import math
import jax
import jax.numpy as jnp
from jax import lax

D = 4096
TOKENS = 4096


def levels(stream_key, dims, cuts, low, largest):
    def one(dim, blocks):
        heights = jax.random.uniform(jax.random.fold_in(jax.random.fold_in(stream_key, 6), dim), (blocks,), jnp.float32, low / len(cuts), largest / len(cuts))
        return jnp.repeat(jnp.exp(heights), dims[dim] // blocks).reshape((-1,) + (1,) * (len(dims) - dim - 1))

    factor_of = one(*cuts[0])
    for cut in cuts[1:]:
        factor_of = factor_of * one(*cut)
    return factor_of


def scatter_about(key, shape, deviation, bound, cuts=(), kind=jnp.bfloat16):
    values = jax.random.normal(key, shape, jnp.float32) * deviation
    if len(cuts) > 0:
        values = levels(key, shape, cuts, -0.22, 0.18) * values
    return jnp.clip(values, min=-bound, max=bound).astype(kind)


def setup_inputs(seed: int = 0) -> dict:
    splits = jax.random.split(jax.random.key(seed), 6)
    return {
        "q_proj": scatter_about(splits[0], (TOKENS, D), 1.0, 6.0, ((0, 32),)),
        "k_proj": scatter_about(splits[1], (TOKENS, D), 1.0, 6.0, ((0, 32),)),
        "v_proj": scatter_about(splits[2], (TOKENS, D), 1.0, 6.0, ((0, 32),)),
        "filter_taps": scatter_about(splits[3], (TOKENS, D), 1.0, 6.0, ((0, 32),)),
        "out_grad": scatter_about(splits[4], (TOKENS, D), 1.0, 6.0, ((0, 32),)),
    }


def reference(q_proj, k_proj, v_proj, filter_taps, out_grad):
    group = math.gcd(D, 256)
    padded = 2 * TOKENS
    norm_scale = 1.0 / math.sqrt(TOKENS)

    def split(array):
        return array.T.reshape(D // group, group, TOKENS)

    def one_group(pieces):
        queries = pieces[0].astype(jnp.float32)
        keys = pieces[1].astype(jnp.float32)
        values = pieces[2].astype(jnp.float32)
        taps = pieces[3].astype(jnp.float32)
        cotangent = pieces[4].astype(jnp.float32)
        gated = lax.optimization_barrier((keys * values).astype(jnp.bfloat16)).astype(jnp.float32)
        back_in = lax.optimization_barrier((cotangent * queries).astype(jnp.bfloat16)).astype(jnp.float32)
        taps_spec = jnp.fft.rfft(taps, padded, axis=-1)
        gated_spec = jnp.fft.rfft(gated, padded, axis=-1)
        back_spec = jnp.fft.rfft(back_in, padded, axis=-1)
        conv_out = norm_scale * jnp.fft.irfft(taps_spec * gated_spec, padded, axis=-1)[:, :TOKENS]
        conv_out = conv_out.astype(jnp.float32)
        mixed = (queries * conv_out).astype(jnp.bfloat16)
        q_grad = (cotangent * conv_out).astype(jnp.bfloat16)
        conv_grad = norm_scale * jnp.fft.irfft(jnp.conj(taps_spec) * back_spec, padded, axis=-1)[:, :TOKENS]
        conv_grad = conv_grad.astype(jnp.float32)
        k_grad = (conv_grad * values).astype(jnp.bfloat16)
        v_grad = (conv_grad * keys).astype(jnp.bfloat16)
        filter_grad = norm_scale * jnp.fft.irfft(back_spec * jnp.conj(gated_spec), padded, axis=-1)[:, :TOKENS]
        filter_grad = filter_grad.astype(jnp.float32).astype(jnp.bfloat16)
        return (mixed, q_grad, k_grad, v_grad, filter_grad)
    results = lax.map(one_group, (split(q_proj), split(k_proj), split(v_proj), split(filter_taps), split(out_grad)))
    mixed = results[0].reshape(D, TOKENS).T
    q_grad = results[1].reshape(D, TOKENS).T
    k_grad = results[2].reshape(D, TOKENS).T
    v_grad = results[3].reshape(D, TOKENS).T
    filter_grad = results[4].reshape(D, TOKENS).T
    return (mixed, q_grad, k_grad, v_grad, filter_grad)
```

```python
import functools
import math

import jax
import jax.numpy as jnp
import numpy as np
from jax import lax
from jax.experimental import pallas as pl
from jax.experimental.pallas import tpu as pltpu
from jax.sharding import PartitionSpec as P

PRECISE = lax.Precision.HIGHEST


def build_tables(first, second):
    points = first * second
    half = first // 2
    rows_first = jnp.arange(first, dtype=jnp.int32)
    rows_half = jnp.arange(half, dtype=jnp.int32)
    rows_second = jnp.arange(second, dtype=jnp.int32)
    outer_phase = rows_first[:, None] * rows_half[None, :] % first
    outer_angle = outer_phase.astype(jnp.float32) * (2.0 * math.pi / first)
    turn_phase = rows_first[:, None] * rows_second[None, :] % points
    turn_angle = turn_phase.astype(jnp.float32) * (2.0 * math.pi / points)
    inner_phase = rows_second[:, None] * rows_second[None, :] % second
    inner_angle = inner_phase.astype(jnp.float32) * (2.0 * math.pi / second)
    return (
        jnp.cos(outer_angle),
        jnp.sin(outer_angle),
        jnp.cos(turn_angle),
        jnp.sin(turn_angle),
        jnp.cos(inner_angle),
        jnp.sin(inner_angle),
    )


def split_table(table):
    upper = table.astype(jnp.bfloat16)
    lower = (table - upper.astype(jnp.float32)).astype(jnp.bfloat16)
    return (upper, lower)


def table_product(table, shaped):
    upper, lower = split_table(table)
    total = jnp.einsum("kn,cnm->ckm", upper, shaped, preferred_element_type=jnp.float32)
    return total + jnp.einsum("kn,cnm->ckm", lower, shaped, preferred_element_type=jnp.float32)


def forward_spectrum(tables, signal):
    outer_cos, outer_sin, turn_cos, turn_sin, inner_cos, inner_sin = tables
    half = outer_cos.shape[1]
    second = inner_cos.shape[0]
    shaped = signal.reshape(signal.shape[0], half, second)
    real_outer = table_product(outer_cos, shaped)
    imag_outer = -table_product(outer_sin, shaped)
    real_turned = real_outer * turn_cos + imag_outer * turn_sin
    imag_turned = imag_outer * turn_cos - real_outer * turn_sin
    real_spec = jnp.einsum(
        "ckn,mn->ckm", real_turned, inner_cos, precision=PRECISE, preferred_element_type=jnp.float32
    )
    real_spec = real_spec + jnp.einsum(
        "ckn,mn->ckm", imag_turned, inner_sin, precision=PRECISE, preferred_element_type=jnp.float32
    )
    imag_spec = jnp.einsum(
        "ckn,mn->ckm", imag_turned, inner_cos, precision=PRECISE, preferred_element_type=jnp.float32
    )
    imag_spec = imag_spec - jnp.einsum(
        "ckn,mn->ckm", real_turned, inner_sin, precision=PRECISE, preferred_element_type=jnp.float32
    )
    return (real_spec, imag_spec)


def inverse_signal(tables, spec_pair):
    outer_cos, outer_sin, turn_cos, turn_sin, inner_cos, inner_sin = tables
    real_spec, imag_spec = spec_pair
    points = outer_cos.shape[0] * inner_cos.shape[0]
    real_inner = jnp.einsum(
        "ckn,mn->ckm", real_spec, inner_cos, precision=PRECISE, preferred_element_type=jnp.float32
    )
    real_inner = real_inner - jnp.einsum(
        "ckn,mn->ckm", imag_spec, inner_sin, precision=PRECISE, preferred_element_type=jnp.float32
    )
    imag_inner = jnp.einsum(
        "ckn,mn->ckm", imag_spec, inner_cos, precision=PRECISE, preferred_element_type=jnp.float32
    )
    imag_inner = imag_inner + jnp.einsum(
        "ckn,mn->ckm", real_spec, inner_sin, precision=PRECISE, preferred_element_type=jnp.float32
    )
    real_turned = real_inner * turn_cos - imag_inner * turn_sin
    imag_turned = imag_inner * turn_cos + real_inner * turn_sin
    result = jnp.einsum(
        "kn,ckm->cnm", outer_cos, real_turned, precision=PRECISE, preferred_element_type=jnp.float32
    )
    result = result - jnp.einsum(
        "kn,ckm->cnm", outer_sin, imag_turned, precision=PRECISE, preferred_element_type=jnp.float32
    )
    return result.reshape(result.shape[0], -1) / points


def product(left_pair, right_pair):
    return (
        left_pair[0] * right_pair[0] - left_pair[1] * right_pair[1],
        left_pair[0] * right_pair[1] + left_pair[1] * right_pair[0],
    )


def product_conj(left_pair, right_pair):
    return (
        left_pair[0] * right_pair[0] + left_pair[1] * right_pair[1],
        left_pair[1] * right_pair[0] - left_pair[0] * right_pair[1],
    )


def forward_inputs(key_rows, value_rows, taps_rows):
    return (
        lax.all_to_all(key_rows, ("ctx", "ch"), split_axis=0, concat_axis=1, tiled=True),
        lax.all_to_all(value_rows, ("ctx", "ch"), split_axis=0, concat_axis=1, tiled=True),
        lax.all_to_all(taps_rows, ("ctx", "ch"), split_axis=0, concat_axis=1, tiled=True),
    )


def backward_inputs(query_rows, grad_rows):
    return (
        lax.all_to_all(query_rows, ("ctx", "ch"), split_axis=0, concat_axis=1, tiled=True),
        lax.all_to_all(grad_rows, ("ctx", "ch"), split_axis=0, concat_axis=1, tiled=True),
    )


def first_outputs(mixed, q_grad):
    moved = (
        lax.all_to_all(mixed, ("ctx", "ch"), split_axis=1, concat_axis=0, tiled=True),
        lax.all_to_all(q_grad, ("ctx", "ch"), split_axis=1, concat_axis=0, tiled=True),
    )
    return tuple((piece.T for piece in moved))


def second_outputs(k_grad, v_grad, filter_grad):
    moved = (
        lax.all_to_all(k_grad, ("ctx", "ch"), split_axis=1, concat_axis=0, tiled=True),
        lax.all_to_all(v_grad, ("ctx", "ch"), split_axis=1, concat_axis=0, tiled=True),
        lax.all_to_all(filter_grad, ("ctx", "ch"), split_axis=1, concat_axis=0, tiled=True),
    )
    return tuple((piece.T for piece in moved))


def general_body(q_proj, k_proj, v_proj, filter_taps, out_grad):
    key_part, value_part, taps_part = forward_inputs(k_proj.T, v_proj.T, filter_taps.T)
    length = key_part.shape[1]
    points = 2 * length
    second = math.gcd(points, 128)
    first = points // second
    tables = build_tables(first, second)
    norm_scale = 1.0 / math.sqrt(length)
    key_wide = key_part.astype(jnp.float32)
    value_wide = value_part.astype(jnp.float32)
    gated = (key_wide * value_wide).astype(jnp.bfloat16)
    gated_spec = forward_spectrum(tables, gated)
    taps_spec = forward_spectrum(tables, taps_part)
    query_part, cotangent = backward_inputs(q_proj.T, out_grad.T)
    query_wide = query_part.astype(jnp.float32)
    grad_wide = cotangent.astype(jnp.float32)
    conv_out = inverse_signal(tables, product(taps_spec, gated_spec)) * norm_scale
    mixed = (query_wide * conv_out).astype(jnp.bfloat16)
    q_grad = (grad_wide * conv_out).astype(jnp.bfloat16)
    mixed, q_grad = first_outputs(mixed, q_grad)
    back_in = (grad_wide * query_wide).astype(jnp.bfloat16)
    back_spec = forward_spectrum(tables, back_in)
    conv_grad = inverse_signal(tables, product_conj(back_spec, taps_spec)) * norm_scale
    filter_grad = (inverse_signal(tables, product_conj(back_spec, gated_spec)) * norm_scale).astype(
        jnp.bfloat16
    )
    k_grad = (conv_grad * value_wide).astype(jnp.bfloat16)
    v_grad = (conv_grad * key_wide).astype(jnp.bfloat16)
    k_grad, v_grad, filter_grad = second_outputs(k_grad, v_grad, filter_grad)
    return (mixed, q_grad, k_grad, v_grad, filter_grad)


MESH_ID = pl.DeviceIdType.MESH
GROUP = 16
BF16 = jnp.bfloat16


def dft_tables(blocks, rows, norm_scale):
    first = 2 * blocks
    points = first * rows
    half = rows // 2
    n1 = np.arange(first)
    outer = np.zeros((first, first))
    outer[0] = 1.0
    outer[1] = np.cos(np.pi * n1)
    for k in range(1, blocks):
        angle = 2.0 * np.pi * (n1 * k % first) / first
        outer[2 * k] = np.cos(angle)
        outer[2 * k + 1] = -np.sin(angle)
    outer_inv = np.linalg.inv(outer)[:blocks] * norm_scale
    outer = outer[:, :blocks]
    n2 = np.arange(rows)
    inner = np.zeros((blocks, 2 * rows, 2 * rows))
    for k in range(1, blocks):
        freq = k + first * np.arange(rows)
        angle = 2.0 * np.pi * (freq[:, None] * n2[None, :] % points) / points
        cos, sin = np.cos(angle), np.sin(angle)
        inner[k] = np.block([[cos, sin], [-sin, cos]])
    for part, k in enumerate((0, blocks)):
        freq = k + first * np.arange(half)
        angle = 2.0 * np.pi * (freq[:, None] * n2[None, :] % points) / points
        columns = slice(part * rows, (part + 1) * rows)
        inner[0, part * half : (part + 1) * half, columns] = np.cos(angle)
        inner[0, rows + part * half : rows + (part + 1) * half, columns] = -np.sin(angle)
    inner[0, rows, :rows] = np.cos(np.pi * n2)
    inner_inv = np.linalg.inv(inner)
    eye = np.eye(GROUP)
    return tuple(
        np.asarray(table, np.float32).astype(BF16)
        for table in (np.kron(outer, eye), inner, inner_inv, np.kron(outer_inv, eye))
    )


def conv_kernel(
    blocks,
    inner_size,
    taps_ref,
    gated_ref,
    back_ref,
    outer_hbm,
    inner_hbm,
    inner_inv_hbm,
    outer_inv_hbm,
    conv_ref,
    cgrad_ref,
    fgrad_ref,
    rx,
    tx,
    mid,
    prod,
    taps_spec,
    gated_spec,
    outer_t,
    inner_t,
    inner_inv_t,
    outer_inv_t,
    table_sem,
    send_sem,
    recv_sem,
):
    rows = taps_ref.shape[0]
    lanes = rx.shape[-1]
    me = lax.axis_index("ctx") * inner_size + lax.axis_index("ch")
    sources = (taps_ref, gated_ref, back_ref)
    results = (conv_ref, cgrad_ref, fgrad_ref)
    tables = (
        (outer_hbm, outer_t),
        (inner_hbm, inner_t),
        (inner_inv_hbm, inner_inv_t),
        (outer_inv_hbm, outer_inv_t),
    )

    def peer_at(step):
        peer = lax.rem(me + step, blocks)
        return peer, (peer // inner_size, lax.rem(peer, inner_size))

    def row_block(index):
        return pl.ds(pl.multiple_of(index * rows, rows), rows)

    def lane_block(index):
        return pl.ds(pl.multiple_of(index * lanes, lanes), lanes)

    def send_in(which):
        pltpu.make_async_copy(
            sources[which].at[:, lane_block(me)], rx.at[which, row_block(me)], recv_sem.at[which]
        ).start()

        @pl.loop(1, blocks)
        def _(step):
            peer, where = peer_at(step)
            pltpu.make_async_remote_copy(
                src_ref=sources[which].at[:, lane_block(peer)],
                dst_ref=rx.at[which, row_block(me)],
                send_sem=send_sem.at[which],
                recv_sem=recv_sem.at[which],
                device_id=where,
                device_id_type=MESH_ID,
            ).start()

    def send_out(which):
        slot = 3 + which
        pltpu.make_async_copy(
            tx.at[which, row_block(me)], results[which].at[:, lane_block(me)], recv_sem.at[slot]
        ).start()

        @pl.loop(1, blocks)
        def _(step):
            peer, where = peer_at(step)
            pltpu.make_async_remote_copy(
                src_ref=tx.at[which, row_block(peer)],
                dst_ref=results[which].at[:, lane_block(me)],
                send_sem=send_sem.at[slot],
                recv_sem=recv_sem.at[slot],
                device_id=where,
                device_id_type=MESH_ID,
            ).start()

    def wait_in(which):
        pltpu.make_async_copy(rx.at[which], rx.at[which], recv_sem.at[which]).wait()

    def wait_out(which):
        pltpu.make_async_copy(results[which], results[which], recv_sem.at[3 + which]).wait()

    def wait_sent(slot):
        part = rx.at[0, pl.ds(0, (blocks - 1) * rows)]
        pltpu.make_async_copy(part, part, send_sem.at[slot]).wait()

    for index, (source, target) in enumerate(tables):
        pltpu.make_async_copy(source, target, table_sem.at[index]).start()

    barrier = pltpu.get_barrier_semaphore()

    @pl.loop(1, blocks)
    def _(step):
        _, where = peer_at(step)
        pl.semaphore_signal(barrier, inc=1, device_id=where, device_id_type=MESH_ID)

    pl.semaphore_wait(barrier, blocks - 1)

    for which in range(3):
        send_in(which)

    for index, (source, target) in enumerate(tables):
        pltpu.make_async_copy(source, target, table_sem.at[index]).wait()

    pairs = rows // (2 * GROUP)

    def outer_stage(which):
        signal = rx.at[which].reshape(blocks, rows, lanes)

        @pl.loop(0, pairs)
        def _(pair):
            low = pl.ds(pl.multiple_of(pair * 2 * GROUP, GROUP), GROUP)
            high = pl.ds(pl.multiple_of(pair * 2 * GROUP + GROUP, GROUP), GROUP)
            data = jnp.concatenate(
                [
                    signal[:, low, :].reshape(blocks * GROUP, lanes),
                    signal[:, high, :].reshape(blocks * GROUP, lanes),
                ],
                axis=1,
            )
            out = jnp.dot(outer_t[...], data, preferred_element_type=jnp.float32).astype(BF16)
            mid[:, low, :] = out[:, :lanes].reshape(2 * blocks, GROUP, lanes)
            mid[:, high, :] = out[:, lanes:].reshape(2 * blocks, GROUP, lanes)

    def spectrum(k):
        data = mid[pl.ds(2 * k, 2)].reshape(2 * rows, lanes)
        return jnp.dot(inner_t[k], data, preferred_element_type=jnp.float32)

    def real_row(k):
        row = lax.broadcasted_iota(jnp.int32, (rows, lanes), 0)
        return jnp.logical_and(row == 0, k == 0)

    def multiply(left, right, alone):
        lr, li = left[:rows], left[rows:]
        rr, ri = right[:rows], right[rows:]
        real, cross = lr * rr, li * ri
        return jnp.concatenate(
            [jnp.where(alone, real, real - cross), jnp.where(alone, cross, lr * ri + li * rr)], axis=0
        ).astype(BF16)

    def multiply_conj(left, right, alone):
        lr, li = left[:rows], left[rows:]
        rr, ri = right[:rows], right[rows:]
        real, cross = lr * rr, li * ri
        return jnp.concatenate(
            [jnp.where(alone, real, real + cross), jnp.where(alone, cross, li * rr - lr * ri)], axis=0
        ).astype(BF16)

    def inverse_outer(which, slot):
        signal = tx.at[which].reshape(blocks, rows, lanes)

        @pl.loop(0, pairs)
        def _(pair):
            low = pl.ds(pl.multiple_of(pair * 2 * GROUP, GROUP), GROUP)
            high = pl.ds(pl.multiple_of(pair * 2 * GROUP + GROUP, GROUP), GROUP)
            data = jnp.concatenate(
                [
                    prod[slot, :, low, :].reshape(2 * blocks * GROUP, lanes),
                    prod[slot, :, high, :].reshape(2 * blocks * GROUP, lanes),
                ],
                axis=1,
            )
            out = jnp.dot(outer_inv_t[...], data, preferred_element_type=jnp.float32).astype(BF16)
            signal[:, low, :] = out[:, :lanes].reshape(blocks, GROUP, lanes)
            signal[:, high, :] = out[:, lanes:].reshape(blocks, GROUP, lanes)

    wait_in(0)
    outer_stage(0)

    @pl.loop(0, blocks)
    def _(k):
        taps_spec[k] = spectrum(k)

    wait_in(1)
    outer_stage(1)

    @pl.loop(0, blocks)
    def _(k):
        spec = spectrum(k)
        gated_spec[k] = spec
        pair = multiply(taps_spec[k], spec, real_row(k))
        out = jnp.dot(inner_inv_t[k], pair, preferred_element_type=jnp.float32)
        prod[0, pl.ds(2 * k, 2)] = out.astype(BF16).reshape(2, rows, lanes)

    inverse_outer(0, 0)
    send_out(0)

    wait_in(2)
    outer_stage(2)

    @pl.loop(0, blocks)
    def _(k):
        spec = spectrum(k)
        alone = real_row(k)
        pair = jnp.concatenate(
            [multiply_conj(spec, taps_spec[k], alone), multiply_conj(spec, gated_spec[k], alone)], axis=1
        )
        out = jnp.dot(inner_inv_t[k], pair, preferred_element_type=jnp.float32).astype(BF16)
        prod[0, pl.ds(2 * k, 2)] = out[:, :lanes].reshape(2, rows, lanes)
        prod[1, pl.ds(2 * k, 2)] = out[:, lanes:].reshape(2, rows, lanes)

    inverse_outer(1, 0)
    send_out(1)
    inverse_outer(2, 1)
    send_out(2)

    for slot in range(6):
        wait_sent(slot)
    for which in range(3):
        wait_out(which)


def convolve(taps, gated, back_in, blocks, inner_size):
    rows, channels = taps.shape
    lanes = channels // blocks
    norm_scale = 1.0 / math.sqrt(rows * blocks)
    tables = dft_tables(blocks, rows, norm_scale)
    signal = jax.ShapeDtypeStruct((rows, channels), BF16)
    anywhere = pl.BlockSpec(memory_space=pl.ANY)
    flops = 2 * lanes * 2 * rows * blocks * (9 * 2 * rows + 6 * blocks * GROUP)
    return pl.pallas_call(
        functools.partial(conv_kernel, blocks, inner_size),
        out_shape=(signal, signal, signal),
        in_specs=[anywhere] * 7,
        out_specs=(anywhere, anywhere, anywhere),
        scratch_shapes=[
            pltpu.VMEM((3, blocks * rows, lanes), BF16),
            pltpu.VMEM((3, blocks * rows, lanes), BF16),
            pltpu.VMEM((2 * blocks, rows, lanes), BF16),
            pltpu.VMEM((2, 2 * blocks, rows, lanes), BF16),
            pltpu.VMEM((blocks, 2 * rows, lanes), jnp.float32),
            pltpu.VMEM((blocks, 2 * rows, lanes), jnp.float32),
        ]
        + [pltpu.VMEM(table.shape, BF16) for table in tables]
        + [
            pltpu.SemaphoreType.DMA((4,)),
            pltpu.SemaphoreType.DMA((6,)),
            pltpu.SemaphoreType.DMA((6,)),
        ],
        compiler_params=pltpu.CompilerParams(
            collective_id=0, has_side_effects=True, vmem_limit_bytes=48 * 1024 * 1024
        ),
        cost_estimate=pl.CostEstimate(flops=flops, bytes_accessed=32 * rows * channels, transcendentals=0),
    )(taps, gated, back_in, *(jnp.asarray(table) for table in tables))


def fast_body(blocks, inner_size, q_proj, k_proj, v_proj, filter_taps, out_grad):
    query = q_proj.astype(jnp.float32)
    key = k_proj.astype(jnp.float32)
    value = v_proj.astype(jnp.float32)
    grad = out_grad.astype(jnp.float32)
    gated = (key * value).astype(BF16)
    back_in = (grad * query).astype(BF16)
    conv_out, conv_grad, filter_grad = convolve(filter_taps, gated, back_in, blocks, inner_size)
    conv_out = conv_out.astype(jnp.float32)
    conv_grad = conv_grad.astype(jnp.float32)
    mixed = (query * conv_out).astype(BF16)
    q_grad = (grad * conv_out).astype(BF16)
    k_grad = (conv_grad * value).astype(BF16)
    v_grad = (conv_grad * key).astype(BF16)
    return (mixed, q_grad, k_grad, v_grad, filter_grad)


def solution(mesh):
    blocks = mesh.shape["ctx"] * mesh.shape["ch"]
    inner_size = mesh.shape["ch"]
    spec = P(("ctx", "ch"), None)

    def run(*arrays):
        tokens, channels = arrays[0].shape
        if channels == 128 * blocks and tokens == 128 * blocks:
            body = functools.partial(fast_body, blocks, inner_size)
        else:
            body = general_body
        return jax.shard_map(
            body, mesh=mesh, in_specs=(spec,) * 5, out_specs=(spec,) * 5, check_vma=False
        )(*arrays)

    return run
```

```python
import functools
import math

import jax
import jax.numpy as jnp
import numpy as np
from jax import lax
from jax.experimental import pallas as pl
from jax.experimental.pallas import tpu as pltpu
from jax.sharding import PartitionSpec as P

PRECISE = lax.Precision.HIGHEST


def build_tables(first, second):
    points = first * second
    half = first // 2
    rows_first = jnp.arange(first, dtype=jnp.int32)
    rows_half = jnp.arange(half, dtype=jnp.int32)
    rows_second = jnp.arange(second, dtype=jnp.int32)
    outer_phase = rows_first[:, None] * rows_half[None, :] % first
    outer_angle = outer_phase.astype(jnp.float32) * (2.0 * math.pi / first)
    turn_phase = rows_first[:, None] * rows_second[None, :] % points
    turn_angle = turn_phase.astype(jnp.float32) * (2.0 * math.pi / points)
    inner_phase = rows_second[:, None] * rows_second[None, :] % second
    inner_angle = inner_phase.astype(jnp.float32) * (2.0 * math.pi / second)
    return (
        jnp.cos(outer_angle),
        jnp.sin(outer_angle),
        jnp.cos(turn_angle),
        jnp.sin(turn_angle),
        jnp.cos(inner_angle),
        jnp.sin(inner_angle),
    )


def split_table(table):
    upper = table.astype(jnp.bfloat16)
    lower = (table - upper.astype(jnp.float32)).astype(jnp.bfloat16)
    return (upper, lower)


def table_product(table, shaped):
    upper, lower = split_table(table)
    total = jnp.einsum("kn,cnm->ckm", upper, shaped, preferred_element_type=jnp.float32)
    return total + jnp.einsum("kn,cnm->ckm", lower, shaped, preferred_element_type=jnp.float32)


def forward_spectrum(tables, signal):
    outer_cos, outer_sin, turn_cos, turn_sin, inner_cos, inner_sin = tables
    half = outer_cos.shape[1]
    second = inner_cos.shape[0]
    shaped = signal.reshape(signal.shape[0], half, second)
    real_outer = table_product(outer_cos, shaped)
    imag_outer = -table_product(outer_sin, shaped)
    real_turned = real_outer * turn_cos + imag_outer * turn_sin
    imag_turned = imag_outer * turn_cos - real_outer * turn_sin
    real_spec = jnp.einsum(
        "ckn,mn->ckm", real_turned, inner_cos, precision=PRECISE, preferred_element_type=jnp.float32
    )
    real_spec = real_spec + jnp.einsum(
        "ckn,mn->ckm", imag_turned, inner_sin, precision=PRECISE, preferred_element_type=jnp.float32
    )
    imag_spec = jnp.einsum(
        "ckn,mn->ckm", imag_turned, inner_cos, precision=PRECISE, preferred_element_type=jnp.float32
    )
    imag_spec = imag_spec - jnp.einsum(
        "ckn,mn->ckm", real_turned, inner_sin, precision=PRECISE, preferred_element_type=jnp.float32
    )
    return (real_spec, imag_spec)


def inverse_signal(tables, spec_pair):
    outer_cos, outer_sin, turn_cos, turn_sin, inner_cos, inner_sin = tables
    real_spec, imag_spec = spec_pair
    points = outer_cos.shape[0] * inner_cos.shape[0]
    real_inner = jnp.einsum(
        "ckn,mn->ckm", real_spec, inner_cos, precision=PRECISE, preferred_element_type=jnp.float32
    )
    real_inner = real_inner - jnp.einsum(
        "ckn,mn->ckm", imag_spec, inner_sin, precision=PRECISE, preferred_element_type=jnp.float32
    )
    imag_inner = jnp.einsum(
        "ckn,mn->ckm", imag_spec, inner_cos, precision=PRECISE, preferred_element_type=jnp.float32
    )
    imag_inner = imag_inner + jnp.einsum(
        "ckn,mn->ckm", real_spec, inner_sin, precision=PRECISE, preferred_element_type=jnp.float32
    )
    real_turned = real_inner * turn_cos - imag_inner * turn_sin
    imag_turned = imag_inner * turn_cos + real_inner * turn_sin
    result = jnp.einsum(
        "kn,ckm->cnm", outer_cos, real_turned, precision=PRECISE, preferred_element_type=jnp.float32
    )
    result = result - jnp.einsum(
        "kn,ckm->cnm", outer_sin, imag_turned, precision=PRECISE, preferred_element_type=jnp.float32
    )
    return result.reshape(result.shape[0], -1) / points


def product(left_pair, right_pair):
    return (
        left_pair[0] * right_pair[0] - left_pair[1] * right_pair[1],
        left_pair[0] * right_pair[1] + left_pair[1] * right_pair[0],
    )


def product_conj(left_pair, right_pair):
    return (
        left_pair[0] * right_pair[0] + left_pair[1] * right_pair[1],
        left_pair[1] * right_pair[0] - left_pair[0] * right_pair[1],
    )


def forward_inputs(key_rows, value_rows, taps_rows):
    return (
        lax.all_to_all(key_rows, ("ctx", "ch"), split_axis=0, concat_axis=1, tiled=True),
        lax.all_to_all(value_rows, ("ctx", "ch"), split_axis=0, concat_axis=1, tiled=True),
        lax.all_to_all(taps_rows, ("ctx", "ch"), split_axis=0, concat_axis=1, tiled=True),
    )


def backward_inputs(query_rows, grad_rows):
    return (
        lax.all_to_all(query_rows, ("ctx", "ch"), split_axis=0, concat_axis=1, tiled=True),
        lax.all_to_all(grad_rows, ("ctx", "ch"), split_axis=0, concat_axis=1, tiled=True),
    )


def first_outputs(mixed, q_grad):
    moved = (
        lax.all_to_all(mixed, ("ctx", "ch"), split_axis=1, concat_axis=0, tiled=True),
        lax.all_to_all(q_grad, ("ctx", "ch"), split_axis=1, concat_axis=0, tiled=True),
    )
    return tuple((piece.T for piece in moved))


def second_outputs(k_grad, v_grad, filter_grad):
    moved = (
        lax.all_to_all(k_grad, ("ctx", "ch"), split_axis=1, concat_axis=0, tiled=True),
        lax.all_to_all(v_grad, ("ctx", "ch"), split_axis=1, concat_axis=0, tiled=True),
        lax.all_to_all(filter_grad, ("ctx", "ch"), split_axis=1, concat_axis=0, tiled=True),
    )
    return tuple((piece.T for piece in moved))


def general_body(q_proj, k_proj, v_proj, filter_taps, out_grad):
    key_part, value_part, taps_part = forward_inputs(k_proj.T, v_proj.T, filter_taps.T)
    length = key_part.shape[1]
    points = 2 * length
    second = math.gcd(points, 128)
    first = points // second
    tables = build_tables(first, second)
    norm_scale = 1.0 / math.sqrt(length)
    key_wide = key_part.astype(jnp.float32)
    value_wide = value_part.astype(jnp.float32)
    gated = (key_wide * value_wide).astype(jnp.bfloat16)
    gated_spec = forward_spectrum(tables, gated)
    taps_spec = forward_spectrum(tables, taps_part)
    query_part, cotangent = backward_inputs(q_proj.T, out_grad.T)
    query_wide = query_part.astype(jnp.float32)
    grad_wide = cotangent.astype(jnp.float32)
    conv_out = inverse_signal(tables, product(taps_spec, gated_spec)) * norm_scale
    mixed = (query_wide * conv_out).astype(jnp.bfloat16)
    q_grad = (grad_wide * conv_out).astype(jnp.bfloat16)
    mixed, q_grad = first_outputs(mixed, q_grad)
    back_in = (grad_wide * query_wide).astype(jnp.bfloat16)
    back_spec = forward_spectrum(tables, back_in)
    conv_grad = inverse_signal(tables, product_conj(back_spec, taps_spec)) * norm_scale
    filter_grad = (inverse_signal(tables, product_conj(back_spec, gated_spec)) * norm_scale).astype(
        jnp.bfloat16
    )
    k_grad = (conv_grad * value_wide).astype(jnp.bfloat16)
    v_grad = (conv_grad * key_wide).astype(jnp.bfloat16)
    k_grad, v_grad, filter_grad = second_outputs(k_grad, v_grad, filter_grad)
    return (mixed, q_grad, k_grad, v_grad, filter_grad)


MESH_ID = pl.DeviceIdType.MESH
GROUP = 16
BF16 = jnp.bfloat16


def dft_tables(blocks, rows, norm_scale):
    first = 2 * blocks
    points = first * rows
    half = rows // 2
    n1 = np.arange(first)
    outer = np.zeros((first, first))
    outer[0] = 1.0
    outer[1] = np.cos(np.pi * n1)
    for k in range(1, blocks):
        angle = 2.0 * np.pi * (n1 * k % first) / first
        outer[2 * k] = np.cos(angle)
        outer[2 * k + 1] = -np.sin(angle)
    outer_inv = np.linalg.inv(outer)[:blocks] * norm_scale
    outer = outer[:, :blocks]
    n2 = np.arange(rows)
    inner = np.zeros((blocks, 2 * rows, 2 * rows))
    for k in range(1, blocks):
        freq = k + first * np.arange(rows)
        angle = 2.0 * np.pi * (freq[:, None] * n2[None, :] % points) / points
        cos, sin = np.cos(angle), np.sin(angle)
        inner[k] = np.block([[cos, sin], [-sin, cos]])
    for part, k in enumerate((0, blocks)):
        freq = k + first * np.arange(half)
        angle = 2.0 * np.pi * (freq[:, None] * n2[None, :] % points) / points
        columns = slice(part * rows, (part + 1) * rows)
        inner[0, part * half : (part + 1) * half, columns] = np.cos(angle)
        inner[0, rows + part * half : rows + (part + 1) * half, columns] = -np.sin(angle)
    inner[0, rows, :rows] = np.cos(np.pi * n2)
    inner_inv = np.linalg.inv(inner)
    eye = np.eye(GROUP)
    return tuple(
        np.asarray(table, np.float32).astype(BF16)
        for table in (np.kron(outer, eye), inner, inner_inv, np.kron(outer_inv, eye))
    )


def conv_kernel(
    blocks,
    inner_size,
    taps_ref,
    key_ref,
    value_ref,
    query_ref,
    grad_ref,
    outer_hbm,
    inner_hbm,
    inner_inv_hbm,
    outer_inv_hbm,
    conv_ref,
    cgrad_ref,
    fgrad_ref,
    rx,
    tx,
    mid,
    prod,
    taps_spec,
    gated_spec,
    back_spec,
    key_v,
    value_v,
    query_v,
    grad_v,
    gated_v,
    back_v,
    outer_t,
    inner_t,
    inner_inv_t,
    outer_inv_t,
    table_sem,
    load_sem,
    send_sem,
    recv_sem,
):
    rows = taps_ref.shape[0]
    lanes = rx.shape[-1]
    me = lax.axis_index("ctx") * inner_size + lax.axis_index("ch")
    sources = (taps_ref, gated_v, back_v)
    loads = ((key_ref, key_v), (value_ref, value_v), (query_ref, query_v), (grad_ref, grad_v))
    results = (conv_ref, cgrad_ref, fgrad_ref)
    tables = (
        (outer_hbm, outer_t),
        (inner_hbm, inner_t),
        (inner_inv_hbm, inner_inv_t),
        (outer_inv_hbm, outer_inv_t),
    )

    def peer_at(step):
        peer = lax.rem(me + step, blocks)
        return peer, (peer // inner_size, lax.rem(peer, inner_size))

    def row_block(index):
        return pl.ds(pl.multiple_of(index * rows, rows), rows)

    def lane_block(index):
        return pl.ds(pl.multiple_of(index * lanes, lanes), lanes)

    def send_in(which):
        pltpu.make_async_copy(
            sources[which].at[:, lane_block(me)], rx.at[which, row_block(me)], recv_sem.at[which]
        ).start()

        @pl.loop(1, blocks)
        def _(step):
            peer, where = peer_at(step)
            pltpu.make_async_remote_copy(
                src_ref=sources[which].at[:, lane_block(peer)],
                dst_ref=rx.at[which, row_block(me)],
                send_sem=send_sem.at[which],
                recv_sem=recv_sem.at[which],
                device_id=where,
                device_id_type=MESH_ID,
            ).start()

    def send_out(which):
        slot = 3 + which
        pltpu.make_async_copy(
            tx.at[which, row_block(me)], results[which].at[:, lane_block(me)], recv_sem.at[slot]
        ).start()

        @pl.loop(1, blocks)
        def _(step):
            peer, where = peer_at(step)
            pltpu.make_async_remote_copy(
                src_ref=tx.at[which, row_block(peer)],
                dst_ref=results[which].at[:, lane_block(me)],
                send_sem=send_sem.at[slot],
                recv_sem=recv_sem.at[slot],
                device_id=where,
                device_id_type=MESH_ID,
            ).start()

    def wait_in(which):
        pltpu.make_async_copy(rx.at[which], rx.at[which], recv_sem.at[which]).wait()

    def wait_out(which):
        pltpu.make_async_copy(results[which], results[which], recv_sem.at[3 + which]).wait()

    def wait_sent(slot):
        part = rx.at[0, pl.ds(0, (blocks - 1) * rows)]
        pltpu.make_async_copy(part, part, send_sem.at[slot]).wait()

    barrier = pltpu.get_barrier_semaphore()

    @pl.loop(1, blocks)
    def _(step):
        _, where = peer_at(step)
        pl.semaphore_signal(barrier, inc=1, device_id=where, device_id_type=MESH_ID)

    for index, (source, target) in enumerate(loads):
        pltpu.make_async_copy(source, target, load_sem.at[index]).start()

    pl.semaphore_wait(barrier, blocks - 1)

    send_in(0)

    def gate(first, second, target):
        for index in (first, second):
            pltpu.make_async_copy(*loads[index], load_sem.at[index]).wait()

        @pl.loop(0, rows // GROUP)
        def _(group):
            part = pl.ds(pl.multiple_of(group * GROUP, GROUP), GROUP)
            left = loads[first][1][part, :].astype(jnp.float32)
            right = loads[second][1][part, :].astype(jnp.float32)
            target[part, :] = (left * right).astype(BF16)

    gate(0, 1, gated_v)
    send_in(1)
    gate(2, 3, back_v)
    send_in(2)

    for index, (source, target) in enumerate(tables):
        pltpu.make_async_copy(source, target, table_sem.at[index]).start()
    for index, (source, target) in enumerate(tables):
        pltpu.make_async_copy(source, target, table_sem.at[index]).wait()

    pairs = rows // (2 * GROUP)

    def outer_stage(which):
        signal = rx.at[which].reshape(blocks, rows, lanes)

        @pl.loop(0, pairs)
        def _(pair):
            low = pl.ds(pl.multiple_of(pair * 2 * GROUP, GROUP), GROUP)
            high = pl.ds(pl.multiple_of(pair * 2 * GROUP + GROUP, GROUP), GROUP)
            data = jnp.concatenate(
                [
                    signal[:, low, :].reshape(blocks * GROUP, lanes),
                    signal[:, high, :].reshape(blocks * GROUP, lanes),
                ],
                axis=1,
            )
            out = jnp.dot(outer_t[...], data, preferred_element_type=jnp.float32).astype(BF16)
            mid[:, low, :] = out[:, :lanes].reshape(2 * blocks, GROUP, lanes)
            mid[:, high, :] = out[:, lanes:].reshape(2 * blocks, GROUP, lanes)

    def spectrum(k):
        data = mid[pl.ds(2 * k, 2)].reshape(2 * rows, lanes)
        return jnp.dot(inner_t[k], data, preferred_element_type=jnp.float32)

    def real_row(k):
        row = lax.broadcasted_iota(jnp.int32, (rows, lanes), 0)
        return jnp.logical_and(row == 0, k == 0)

    def multiply(left, right, alone):
        lr, li = left[:rows], left[rows:]
        rr, ri = right[:rows], right[rows:]
        real, cross = lr * rr, li * ri
        return jnp.concatenate(
            [jnp.where(alone, real, real - cross), jnp.where(alone, cross, lr * ri + li * rr)], axis=0
        ).astype(BF16)

    def multiply_conj(left, right, alone):
        lr, li = left[:rows], left[rows:]
        rr, ri = right[:rows], right[rows:]
        real, cross = lr * rr, li * ri
        return jnp.concatenate(
            [jnp.where(alone, real, real + cross), jnp.where(alone, cross, li * rr - lr * ri)], axis=0
        ).astype(BF16)

    def inverse_outer(which):
        signal = tx.at[which].reshape(blocks, rows, lanes)

        @pl.loop(0, pairs)
        def _(pair):
            low = pl.ds(pl.multiple_of(pair * 2 * GROUP, GROUP), GROUP)
            high = pl.ds(pl.multiple_of(pair * 2 * GROUP + GROUP, GROUP), GROUP)
            data = jnp.concatenate(
                [
                    prod[:, low, :].reshape(2 * blocks * GROUP, lanes),
                    prod[:, high, :].reshape(2 * blocks * GROUP, lanes),
                ],
                axis=1,
            )
            out = jnp.dot(outer_inv_t[...], data, preferred_element_type=jnp.float32).astype(BF16)
            signal[:, low, :] = out[:, :lanes].reshape(blocks, GROUP, lanes)
            signal[:, high, :] = out[:, lanes:].reshape(blocks, GROUP, lanes)

    def invert(k, pair):
        out = jnp.dot(inner_inv_t[k], pair, preferred_element_type=jnp.float32)
        prod[pl.ds(2 * k, 2)] = out.astype(BF16).reshape(2, rows, lanes)

    wait_in(0)
    outer_stage(0)

    @pl.loop(0, blocks, unroll=2)
    def _(k):
        taps_spec[k] = spectrum(k)

    wait_in(1)
    outer_stage(1)

    @pl.loop(0, blocks, unroll=2)
    def _(k):
        spec = spectrum(k)
        gated_spec[k] = spec
        invert(k, multiply(taps_spec[k], spec, real_row(k)))

    inverse_outer(0)
    send_out(0)

    wait_in(2)
    outer_stage(2)

    @pl.loop(0, blocks, unroll=2)
    def _(k):
        spec = spectrum(k)
        back_spec[k] = spec
        invert(k, multiply_conj(spec, taps_spec[k], real_row(k)))

    inverse_outer(1)
    send_out(1)

    @pl.loop(0, blocks, unroll=2)
    def _(k):
        invert(k, multiply_conj(back_spec[k], gated_spec[k], real_row(k)))

    inverse_outer(2)
    send_out(2)

    for slot in range(6):
        wait_sent(slot)
    for which in range(3):
        wait_out(which)


def convolve(taps, key, value, query, grad, blocks, inner_size):
    rows, channels = taps.shape
    lanes = channels // blocks
    norm_scale = 1.0 / math.sqrt(rows * blocks)
    tables = dft_tables(blocks, rows, norm_scale)
    signal = jax.ShapeDtypeStruct((rows, channels), BF16)
    anywhere = pl.BlockSpec(memory_space=pl.ANY)
    flops = 2 * lanes * 2 * rows * blocks * (9 * 2 * rows + 6 * blocks * GROUP)
    return pl.pallas_call(
        functools.partial(conv_kernel, blocks, inner_size),
        out_shape=(signal, signal, signal),
        in_specs=[pl.BlockSpec(memory_space=pltpu.HBM)] * 9,
        out_specs=(anywhere, anywhere, anywhere),
        scratch_shapes=[
            pltpu.VMEM((3, blocks * rows, lanes), BF16),
            pltpu.VMEM((3, blocks * rows, lanes), BF16),
            pltpu.VMEM((2 * blocks, rows, lanes), BF16),
            pltpu.VMEM((2 * blocks, rows, lanes), BF16),
            pltpu.VMEM((blocks, 2 * rows, lanes), jnp.float32),
            pltpu.VMEM((blocks, 2 * rows, lanes), jnp.float32),
            pltpu.VMEM((blocks, 2 * rows, lanes), jnp.float32),
        ]
        + [pltpu.VMEM((rows, channels), BF16)] * 6
        + [pltpu.VMEM(table.shape, BF16) for table in tables]
        + [
            pltpu.SemaphoreType.DMA((4,)),
            pltpu.SemaphoreType.DMA((4,)),
            pltpu.SemaphoreType.DMA((6,)),
            pltpu.SemaphoreType.DMA((6,)),
        ],
        compiler_params=pltpu.CompilerParams(
            collective_id=0, has_side_effects=True, vmem_limit_bytes=48 * 1024 * 1024
        ),
        cost_estimate=pl.CostEstimate(flops=flops, bytes_accessed=32 * rows * channels, transcendentals=0),
    )(taps, key, value, query, grad, *(jnp.asarray(table) for table in tables))


def fast_body(blocks, inner_size, q_proj, k_proj, v_proj, filter_taps, out_grad):
    query = q_proj.astype(jnp.float32)
    key = k_proj.astype(jnp.float32)
    value = v_proj.astype(jnp.float32)
    grad = out_grad.astype(jnp.float32)
    conv_out, conv_grad, filter_grad = convolve(
        filter_taps, k_proj, v_proj, q_proj, out_grad, blocks, inner_size
    )
    conv_out = conv_out.astype(jnp.float32)
    conv_grad = conv_grad.astype(jnp.float32)
    mixed = (query * conv_out).astype(BF16)
    q_grad = (grad * conv_out).astype(BF16)
    k_grad = (conv_grad * value).astype(BF16)
    v_grad = (conv_grad * key).astype(BF16)
    return (mixed, q_grad, k_grad, v_grad, filter_grad)


def solution(mesh):
    blocks = mesh.shape["ctx"] * mesh.shape["ch"]
    inner_size = mesh.shape["ch"]
    spec = P(("ctx", "ch"), None)

    def run(*arrays):
        tokens, channels = arrays[0].shape
        if channels == 128 * blocks and tokens == 128 * blocks:
            body = functools.partial(fast_body, blocks, inner_size)
        else:
            body = general_body
        return jax.shard_map(
            body, mesh=mesh, in_specs=(spec,) * 5, out_specs=(spec,) * 5, check_vma=False
        )(*arrays)

    return run
```

```python
import functools
import math

import jax
import jax.numpy as jnp
import numpy as np
from jax import lax
from jax.experimental import pallas as pl
from jax.experimental.pallas import tpu as pltpu
from jax.sharding import PartitionSpec as P

PRECISE = lax.Precision.HIGHEST


def build_tables(first, second):
    points = first * second
    half = first // 2
    rows_first = jnp.arange(first, dtype=jnp.int32)
    rows_half = jnp.arange(half, dtype=jnp.int32)
    rows_second = jnp.arange(second, dtype=jnp.int32)
    outer_phase = rows_first[:, None] * rows_half[None, :] % first
    outer_angle = outer_phase.astype(jnp.float32) * (2.0 * math.pi / first)
    turn_phase = rows_first[:, None] * rows_second[None, :] % points
    turn_angle = turn_phase.astype(jnp.float32) * (2.0 * math.pi / points)
    inner_phase = rows_second[:, None] * rows_second[None, :] % second
    inner_angle = inner_phase.astype(jnp.float32) * (2.0 * math.pi / second)
    return (
        jnp.cos(outer_angle),
        jnp.sin(outer_angle),
        jnp.cos(turn_angle),
        jnp.sin(turn_angle),
        jnp.cos(inner_angle),
        jnp.sin(inner_angle),
    )


def split_table(table):
    upper = table.astype(jnp.bfloat16)
    lower = (table - upper.astype(jnp.float32)).astype(jnp.bfloat16)
    return (upper, lower)


def table_product(table, shaped):
    upper, lower = split_table(table)
    total = jnp.einsum("kn,cnm->ckm", upper, shaped, preferred_element_type=jnp.float32)
    return total + jnp.einsum("kn,cnm->ckm", lower, shaped, preferred_element_type=jnp.float32)


def forward_spectrum(tables, signal):
    outer_cos, outer_sin, turn_cos, turn_sin, inner_cos, inner_sin = tables
    half = outer_cos.shape[1]
    second = inner_cos.shape[0]
    shaped = signal.reshape(signal.shape[0], half, second)
    real_outer = table_product(outer_cos, shaped)
    imag_outer = -table_product(outer_sin, shaped)
    real_turned = real_outer * turn_cos + imag_outer * turn_sin
    imag_turned = imag_outer * turn_cos - real_outer * turn_sin
    real_spec = jnp.einsum(
        "ckn,mn->ckm", real_turned, inner_cos, precision=PRECISE, preferred_element_type=jnp.float32
    )
    real_spec = real_spec + jnp.einsum(
        "ckn,mn->ckm", imag_turned, inner_sin, precision=PRECISE, preferred_element_type=jnp.float32
    )
    imag_spec = jnp.einsum(
        "ckn,mn->ckm", imag_turned, inner_cos, precision=PRECISE, preferred_element_type=jnp.float32
    )
    imag_spec = imag_spec - jnp.einsum(
        "ckn,mn->ckm", real_turned, inner_sin, precision=PRECISE, preferred_element_type=jnp.float32
    )
    return (real_spec, imag_spec)


def inverse_signal(tables, spec_pair):
    outer_cos, outer_sin, turn_cos, turn_sin, inner_cos, inner_sin = tables
    real_spec, imag_spec = spec_pair
    points = outer_cos.shape[0] * inner_cos.shape[0]
    real_inner = jnp.einsum(
        "ckn,mn->ckm", real_spec, inner_cos, precision=PRECISE, preferred_element_type=jnp.float32
    )
    real_inner = real_inner - jnp.einsum(
        "ckn,mn->ckm", imag_spec, inner_sin, precision=PRECISE, preferred_element_type=jnp.float32
    )
    imag_inner = jnp.einsum(
        "ckn,mn->ckm", imag_spec, inner_cos, precision=PRECISE, preferred_element_type=jnp.float32
    )
    imag_inner = imag_inner + jnp.einsum(
        "ckn,mn->ckm", real_spec, inner_sin, precision=PRECISE, preferred_element_type=jnp.float32
    )
    real_turned = real_inner * turn_cos - imag_inner * turn_sin
    imag_turned = imag_inner * turn_cos + real_inner * turn_sin
    result = jnp.einsum(
        "kn,ckm->cnm", outer_cos, real_turned, precision=PRECISE, preferred_element_type=jnp.float32
    )
    result = result - jnp.einsum(
        "kn,ckm->cnm", outer_sin, imag_turned, precision=PRECISE, preferred_element_type=jnp.float32
    )
    return result.reshape(result.shape[0], -1) / points


def product(left_pair, right_pair):
    return (
        left_pair[0] * right_pair[0] - left_pair[1] * right_pair[1],
        left_pair[0] * right_pair[1] + left_pair[1] * right_pair[0],
    )


def product_conj(left_pair, right_pair):
    return (
        left_pair[0] * right_pair[0] + left_pair[1] * right_pair[1],
        left_pair[1] * right_pair[0] - left_pair[0] * right_pair[1],
    )


def forward_inputs(key_rows, value_rows, taps_rows):
    return (
        lax.all_to_all(key_rows, ("ctx", "ch"), split_axis=0, concat_axis=1, tiled=True),
        lax.all_to_all(value_rows, ("ctx", "ch"), split_axis=0, concat_axis=1, tiled=True),
        lax.all_to_all(taps_rows, ("ctx", "ch"), split_axis=0, concat_axis=1, tiled=True),
    )


def backward_inputs(query_rows, grad_rows):
    return (
        lax.all_to_all(query_rows, ("ctx", "ch"), split_axis=0, concat_axis=1, tiled=True),
        lax.all_to_all(grad_rows, ("ctx", "ch"), split_axis=0, concat_axis=1, tiled=True),
    )


def first_outputs(mixed, q_grad):
    moved = (
        lax.all_to_all(mixed, ("ctx", "ch"), split_axis=1, concat_axis=0, tiled=True),
        lax.all_to_all(q_grad, ("ctx", "ch"), split_axis=1, concat_axis=0, tiled=True),
    )
    return tuple((piece.T for piece in moved))


def second_outputs(k_grad, v_grad, filter_grad):
    moved = (
        lax.all_to_all(k_grad, ("ctx", "ch"), split_axis=1, concat_axis=0, tiled=True),
        lax.all_to_all(v_grad, ("ctx", "ch"), split_axis=1, concat_axis=0, tiled=True),
        lax.all_to_all(filter_grad, ("ctx", "ch"), split_axis=1, concat_axis=0, tiled=True),
    )
    return tuple((piece.T for piece in moved))


def general_body(q_proj, k_proj, v_proj, filter_taps, out_grad):
    key_part, value_part, taps_part = forward_inputs(k_proj.T, v_proj.T, filter_taps.T)
    length = key_part.shape[1]
    points = 2 * length
    second = math.gcd(points, 128)
    first = points // second
    tables = build_tables(first, second)
    norm_scale = 1.0 / math.sqrt(length)
    key_wide = key_part.astype(jnp.float32)
    value_wide = value_part.astype(jnp.float32)
    gated = (key_wide * value_wide).astype(jnp.bfloat16)
    gated_spec = forward_spectrum(tables, gated)
    taps_spec = forward_spectrum(tables, taps_part)
    query_part, cotangent = backward_inputs(q_proj.T, out_grad.T)
    query_wide = query_part.astype(jnp.float32)
    grad_wide = cotangent.astype(jnp.float32)
    conv_out = inverse_signal(tables, product(taps_spec, gated_spec)) * norm_scale
    mixed = (query_wide * conv_out).astype(jnp.bfloat16)
    q_grad = (grad_wide * conv_out).astype(jnp.bfloat16)
    mixed, q_grad = first_outputs(mixed, q_grad)
    back_in = (grad_wide * query_wide).astype(jnp.bfloat16)
    back_spec = forward_spectrum(tables, back_in)
    conv_grad = inverse_signal(tables, product_conj(back_spec, taps_spec)) * norm_scale
    filter_grad = (inverse_signal(tables, product_conj(back_spec, gated_spec)) * norm_scale).astype(
        jnp.bfloat16
    )
    k_grad = (conv_grad * value_wide).astype(jnp.bfloat16)
    v_grad = (conv_grad * key_wide).astype(jnp.bfloat16)
    k_grad, v_grad, filter_grad = second_outputs(k_grad, v_grad, filter_grad)
    return (mixed, q_grad, k_grad, v_grad, filter_grad)


MESH_ID = pl.DeviceIdType.MESH
GROUP = 16
VMEM_MIB = 57
BF16 = jnp.bfloat16


def dft_tables(blocks, rows, norm_scale):
    first = 2 * blocks
    points = first * rows
    half = rows // 2
    n1 = np.arange(first)
    outer = np.zeros((first, first))
    outer[0] = 1.0
    outer[1] = np.cos(np.pi * n1)
    for k in range(1, blocks):
        angle = 2.0 * np.pi * (n1 * k % first) / first
        outer[2 * k] = np.cos(angle)
        outer[2 * k + 1] = -np.sin(angle)
    outer_inv = np.linalg.inv(outer)[:blocks] * norm_scale
    outer = outer[:, :blocks]
    n2 = np.arange(rows)
    inner = np.zeros((blocks, 2 * rows, 2 * rows))
    for k in range(1, blocks):
        freq = k + first * np.arange(rows)
        angle = 2.0 * np.pi * (freq[:, None] * n2[None, :] % points) / points
        cos, sin = np.cos(angle), np.sin(angle)
        inner[k] = np.block([[cos, sin], [-sin, cos]])
    for part, k in enumerate((0, blocks)):
        freq = k + first * np.arange(half)
        angle = 2.0 * np.pi * (freq[:, None] * n2[None, :] % points) / points
        columns = slice(part * rows, (part + 1) * rows)
        inner[0, part * half : (part + 1) * half, columns] = np.cos(angle)
        inner[0, rows + part * half : rows + (part + 1) * half, columns] = -np.sin(angle)
    inner[0, rows, :rows] = np.cos(np.pi * n2)
    inner_inv = np.linalg.inv(inner)
    eye = np.eye(GROUP)
    return tuple(
        np.asarray(table, np.float32).astype(BF16)
        for table in (np.kron(outer, eye), inner, inner_inv, np.kron(outer_inv, eye))
    )


def conv_kernel(
    blocks,
    inner_size,
    taps_ref,
    key_ref,
    value_ref,
    query_ref,
    grad_ref,
    outer_hbm,
    inner_hbm,
    inner_inv_hbm,
    outer_inv_hbm,
    mixed_ref,
    qgrad_ref,
    kgrad_ref,
    vgrad_ref,
    fgrad_ref,
    rx,
    tx,
    mid,
    prod,
    taps_spec,
    gated_spec,
    back_spec,
    key_v,
    value_v,
    query_v,
    grad_v,
    gated_v,
    back_v,
    conv_v,
    cgrad_v,
    outer_t,
    inner_t,
    inner_inv_t,
    outer_inv_t,
    table_sem,
    load_sem,
    store_sem,
    send_sem,
    recv_sem,
):
    rows = taps_ref.shape[0]
    lanes = rx.shape[-1]
    me = lax.axis_index("ctx") * inner_size + lax.axis_index("ch")
    sources = (taps_ref, gated_v, back_v)
    loads = ((key_ref, key_v), (value_ref, value_v), (query_ref, query_v), (grad_ref, grad_v))
    results = (conv_v, cgrad_v, fgrad_ref)
    tables = (
        (outer_hbm, outer_t),
        (inner_hbm, inner_t),
        (inner_inv_hbm, inner_inv_t),
        (outer_inv_hbm, outer_inv_t),
    )

    def peer_at(step):
        peer = lax.rem(me + step, blocks)
        return peer, (peer // inner_size, lax.rem(peer, inner_size))

    def row_block(index):
        return pl.ds(pl.multiple_of(index * rows, rows), rows)

    def lane_block(index):
        return pl.ds(pl.multiple_of(index * lanes, lanes), lanes)

    def send_in(which):
        pltpu.make_async_copy(
            sources[which].at[:, lane_block(me)], rx.at[which, row_block(me)], recv_sem.at[which]
        ).start()

        @pl.loop(1, blocks)
        def _(step):
            peer, where = peer_at(step)
            pltpu.make_async_remote_copy(
                src_ref=sources[which].at[:, lane_block(peer)],
                dst_ref=rx.at[which, row_block(me)],
                send_sem=send_sem.at[which],
                recv_sem=recv_sem.at[which],
                device_id=where,
                device_id_type=MESH_ID,
            ).start()

    def send_out(which):
        slot = 3 + which
        pltpu.make_async_copy(
            tx.at[which, row_block(me)], results[which].at[:, lane_block(me)], recv_sem.at[slot]
        ).start()

        @pl.loop(1, blocks)
        def _(step):
            peer, where = peer_at(step)
            pltpu.make_async_remote_copy(
                src_ref=tx.at[which, row_block(peer)],
                dst_ref=results[which].at[:, lane_block(me)],
                send_sem=send_sem.at[slot],
                recv_sem=recv_sem.at[slot],
                device_id=where,
                device_id_type=MESH_ID,
            ).start()

    def wait_in(which):
        pltpu.make_async_copy(rx.at[which], rx.at[which], recv_sem.at[which]).wait()

    def wait_out(which):
        pltpu.make_async_copy(results[which], results[which], recv_sem.at[3 + which]).wait()

    def wait_sent(slot):
        part = rx.at[0, pl.ds(0, (blocks - 1) * rows)]
        pltpu.make_async_copy(part, part, send_sem.at[slot]).wait()

    barrier = pltpu.get_barrier_semaphore()

    @pl.loop(1, blocks)
    def _(step):
        _, where = peer_at(step)
        pl.semaphore_signal(barrier, inc=1, device_id=where, device_id_type=MESH_ID)

    for index, (source, target) in enumerate(loads):
        pltpu.make_async_copy(source, target, load_sem.at[index]).start()

    pl.semaphore_wait(barrier, blocks - 1)

    send_in(0)

    def gate(first, second, target):
        for index in (first, second):
            pltpu.make_async_copy(*loads[index], load_sem.at[index]).wait()

        @pl.loop(0, rows // GROUP)
        def _(group):
            part = pl.ds(pl.multiple_of(group * GROUP, GROUP), GROUP)
            left = loads[first][1][part, :].astype(jnp.float32)
            right = loads[second][1][part, :].astype(jnp.float32)
            target[part, :] = (left * right).astype(BF16)

    gate(0, 1, gated_v)
    send_in(1)
    gate(2, 3, back_v)
    send_in(2)

    for index, (source, target) in enumerate(tables):
        pltpu.make_async_copy(source, target, table_sem.at[index]).start()
    for index, (source, target) in enumerate(tables):
        pltpu.make_async_copy(source, target, table_sem.at[index]).wait()

    pairs = rows // (2 * GROUP)

    def outer_stage(which):
        signal = rx.at[which].reshape(blocks, rows, lanes)

        @pl.loop(0, pairs)
        def _(pair):
            low = pl.ds(pl.multiple_of(pair * 2 * GROUP, GROUP), GROUP)
            high = pl.ds(pl.multiple_of(pair * 2 * GROUP + GROUP, GROUP), GROUP)
            data = jnp.concatenate(
                [
                    signal[:, low, :].reshape(blocks * GROUP, lanes),
                    signal[:, high, :].reshape(blocks * GROUP, lanes),
                ],
                axis=1,
            )
            out = jnp.dot(outer_t[...], data, preferred_element_type=jnp.float32).astype(BF16)
            mid[:, low, :] = out[:, :lanes].reshape(2 * blocks, GROUP, lanes)
            mid[:, high, :] = out[:, lanes:].reshape(2 * blocks, GROUP, lanes)

    def spectrum(k):
        data = mid[pl.ds(2 * k, 2)].reshape(2 * rows, lanes)
        return jnp.dot(inner_t[k], data, preferred_element_type=jnp.float32)

    def real_row(k):
        row = lax.broadcasted_iota(jnp.int32, (rows, lanes), 0)
        return jnp.logical_and(row == 0, k == 0)

    def multiply(left, right, alone):
        lr, li = left[:rows], left[rows:]
        rr, ri = right[:rows], right[rows:]
        real, cross = lr * rr, li * ri
        return jnp.concatenate(
            [jnp.where(alone, real, real - cross), jnp.where(alone, cross, lr * ri + li * rr)], axis=0
        ).astype(BF16)

    def multiply_conj(left, right, alone):
        lr, li = left[:rows], left[rows:]
        rr, ri = right[:rows], right[rows:]
        real, cross = lr * rr, li * ri
        return jnp.concatenate(
            [jnp.where(alone, real, real + cross), jnp.where(alone, cross, li * rr - lr * ri)], axis=0
        ).astype(BF16)

    def inverse_outer(which):
        signal = tx.at[which].reshape(blocks, rows, lanes)

        @pl.loop(0, pairs)
        def _(pair):
            low = pl.ds(pl.multiple_of(pair * 2 * GROUP, GROUP), GROUP)
            high = pl.ds(pl.multiple_of(pair * 2 * GROUP + GROUP, GROUP), GROUP)
            data = jnp.concatenate(
                [
                    prod[:, low, :].reshape(2 * blocks * GROUP, lanes),
                    prod[:, high, :].reshape(2 * blocks * GROUP, lanes),
                ],
                axis=1,
            )
            out = jnp.dot(outer_inv_t[...], data, preferred_element_type=jnp.float32).astype(BF16)
            signal[:, low, :] = out[:, :lanes].reshape(blocks, GROUP, lanes)
            signal[:, high, :] = out[:, lanes:].reshape(blocks, GROUP, lanes)

    def invert(k, pair):
        out = jnp.dot(inner_inv_t[k], pair, preferred_element_type=jnp.float32)
        prod[pl.ds(2 * k, 2)] = out.astype(BF16).reshape(2, rows, lanes)

    wait_in(0)
    outer_stage(0)

    @pl.loop(0, blocks, unroll=2)
    def _(k):
        taps_spec[k] = spectrum(k)

    wait_in(1)
    outer_stage(1)

    @pl.loop(0, blocks, unroll=2)
    def _(k):
        spec = spectrum(k)
        gated_spec[k] = spec
        invert(k, multiply(taps_spec[k], spec, real_row(k)))

    inverse_outer(0)
    send_out(0)

    wait_in(2)
    outer_stage(2)

    @pl.loop(0, blocks, unroll=2)
    def _(k):
        spec = spectrum(k)
        back_spec[k] = spec
        invert(k, multiply_conj(spec, taps_spec[k], real_row(k)))

    inverse_outer(1)
    send_out(1)

    @pl.loop(0, blocks, unroll=2)
    def _(k):
        invert(k, multiply_conj(back_spec[k], gated_spec[k], real_row(k)))

    inverse_outer(2)
    send_out(2)

    def products(which, first, second):
        wait_out(which)
        source = results[which]

        @pl.loop(0, rows // GROUP)
        def _(group):
            part = pl.ds(pl.multiple_of(group * GROUP, GROUP), GROUP)
            conv = source[part, :].astype(jnp.float32)
            for buffer, _, _ in (first, second):
                buffer[part, :] = (buffer[part, :].astype(jnp.float32) * conv).astype(BF16)

        for buffer, target, index in (first, second):
            pltpu.make_async_copy(buffer, target, store_sem.at[index]).start()

    stores = (
        (query_v, mixed_ref, 0),
        (grad_v, qgrad_ref, 1),
        (value_v, kgrad_ref, 2),
        (key_v, vgrad_ref, 3),
    )
    products(0, stores[0], stores[1])
    products(1, stores[2], stores[3])

    for slot in range(6):
        wait_sent(slot)
    for buffer, target, index in stores:
        pltpu.make_async_copy(buffer, target, store_sem.at[index]).wait()
    wait_out(2)


def place_kernel(parts, *refs):
    count = len(refs) // 2
    sources, targets, sem = refs[:count], refs[count:-1], refs[-1]
    size = sources[0].shape[0] // parts
    copies = [
        pltpu.make_async_copy(
            sources[which].at[pl.ds(part * size, size)],
            targets[which].at[pl.ds(part * size, size)],
            sem.at[which * parts + part],
        )
        for part in range(parts)
        for which in range(count)
    ]
    for copy in copies:
        copy.start()
    for copy in copies:
        copy.wait()


def place(results):
    anywhere = pl.BlockSpec(memory_space=pl.ANY)
    count, parts = len(results), 4
    return pl.pallas_call(
        functools.partial(place_kernel, parts),
        out_shape=tuple(jax.ShapeDtypeStruct(result.shape, result.dtype) for result in results),
        in_specs=[anywhere] * count,
        out_specs=(anywhere,) * count,
        scratch_shapes=[pltpu.SemaphoreType.DMA((count * parts,))],
    )(*results)


def convolve(taps, key, value, query, grad, blocks, inner_size):
    rows, channels = taps.shape
    lanes = channels // blocks
    norm_scale = 1.0 / math.sqrt(rows * blocks)
    tables = dft_tables(blocks, rows, norm_scale)
    signal = jax.ShapeDtypeStruct((rows, channels), BF16)
    anywhere = pl.BlockSpec(memory_space=pl.ANY)
    flops = 2 * lanes * 2 * rows * blocks * (9 * 2 * rows + 6 * blocks * GROUP)
    return pl.pallas_call(
        functools.partial(conv_kernel, blocks, inner_size),
        out_shape=(signal,) * 5,
        in_specs=[pl.BlockSpec(memory_space=pltpu.HBM)] * 9,
        out_specs=(anywhere,) * 5,
        scratch_shapes=[
            pltpu.VMEM((3, blocks * rows, lanes), BF16),
            pltpu.VMEM((3, blocks * rows, lanes), BF16),
            pltpu.VMEM((2 * blocks, rows, lanes), BF16),
            pltpu.VMEM((2 * blocks, rows, lanes), BF16),
            pltpu.VMEM((blocks, 2 * rows, lanes), jnp.float32),
            pltpu.VMEM((blocks, 2 * rows, lanes), jnp.float32),
            pltpu.VMEM((blocks, 2 * rows, lanes), jnp.float32),
        ]
        + [pltpu.VMEM((rows, channels), BF16)] * 8
        + [pltpu.VMEM(table.shape, BF16) for table in tables]
        + [
            pltpu.SemaphoreType.DMA((4,)),
            pltpu.SemaphoreType.DMA((4,)),
            pltpu.SemaphoreType.DMA((4,)),
            pltpu.SemaphoreType.DMA((6,)),
            pltpu.SemaphoreType.DMA((6,)),
        ],
        compiler_params=pltpu.CompilerParams(
            collective_id=0, has_side_effects=True, vmem_limit_bytes=VMEM_MIB * 1024 * 1024
        ),
        cost_estimate=pl.CostEstimate(flops=flops, bytes_accessed=32 * rows * channels, transcendentals=0),
    )(taps, key, value, query, grad, *(jnp.asarray(table) for table in tables))


def fast_body(blocks, inner_size, q_proj, k_proj, v_proj, filter_taps, out_grad):
    return place(convolve(filter_taps, k_proj, v_proj, q_proj, out_grad, blocks, inner_size))


def solution(mesh):
    blocks = mesh.shape["ctx"] * mesh.shape["ch"]
    inner_size = mesh.shape["ch"]
    spec = P(("ctx", "ch"), None)

    def run(*arrays):
        tokens, channels = arrays[0].shape
        if channels == 128 * blocks and tokens == 128 * blocks:
            body = functools.partial(fast_body, blocks, inner_size)
        else:
            body = general_body
        return jax.shard_map(
            body, mesh=mesh, in_specs=(spec,) * 5, out_specs=(spec,) * 5, check_vma=False
        )(*arrays)

    return run
```

```python
import functools
import math

import jax
import jax.numpy as jnp
import numpy as np
from jax import lax
from jax.experimental import pallas as pl
from jax.experimental.pallas import tpu as pltpu
from jax.sharding import PartitionSpec as P

PRECISE = lax.Precision.HIGHEST


def build_tables(first, second):
    points = first * second
    half = first // 2
    rows_first = jnp.arange(first, dtype=jnp.int32)
    rows_half = jnp.arange(half, dtype=jnp.int32)
    rows_second = jnp.arange(second, dtype=jnp.int32)
    outer_phase = rows_first[:, None] * rows_half[None, :] % first
    outer_angle = outer_phase.astype(jnp.float32) * (2.0 * math.pi / first)
    turn_phase = rows_first[:, None] * rows_second[None, :] % points
    turn_angle = turn_phase.astype(jnp.float32) * (2.0 * math.pi / points)
    inner_phase = rows_second[:, None] * rows_second[None, :] % second
    inner_angle = inner_phase.astype(jnp.float32) * (2.0 * math.pi / second)
    return (
        jnp.cos(outer_angle),
        jnp.sin(outer_angle),
        jnp.cos(turn_angle),
        jnp.sin(turn_angle),
        jnp.cos(inner_angle),
        jnp.sin(inner_angle),
    )


def split_table(table):
    upper = table.astype(jnp.bfloat16)
    lower = (table - upper.astype(jnp.float32)).astype(jnp.bfloat16)
    return (upper, lower)


def table_product(table, shaped):
    upper, lower = split_table(table)
    total = jnp.einsum("kn,cnm->ckm", upper, shaped, preferred_element_type=jnp.float32)
    return total + jnp.einsum("kn,cnm->ckm", lower, shaped, preferred_element_type=jnp.float32)


def forward_spectrum(tables, signal):
    outer_cos, outer_sin, turn_cos, turn_sin, inner_cos, inner_sin = tables
    half = outer_cos.shape[1]
    second = inner_cos.shape[0]
    shaped = signal.reshape(signal.shape[0], half, second)
    real_outer = table_product(outer_cos, shaped)
    imag_outer = -table_product(outer_sin, shaped)
    real_turned = real_outer * turn_cos + imag_outer * turn_sin
    imag_turned = imag_outer * turn_cos - real_outer * turn_sin
    real_spec = jnp.einsum(
        "ckn,mn->ckm", real_turned, inner_cos, precision=PRECISE, preferred_element_type=jnp.float32
    )
    real_spec = real_spec + jnp.einsum(
        "ckn,mn->ckm", imag_turned, inner_sin, precision=PRECISE, preferred_element_type=jnp.float32
    )
    imag_spec = jnp.einsum(
        "ckn,mn->ckm", imag_turned, inner_cos, precision=PRECISE, preferred_element_type=jnp.float32
    )
    imag_spec = imag_spec - jnp.einsum(
        "ckn,mn->ckm", real_turned, inner_sin, precision=PRECISE, preferred_element_type=jnp.float32
    )
    return (real_spec, imag_spec)


def inverse_signal(tables, spec_pair):
    outer_cos, outer_sin, turn_cos, turn_sin, inner_cos, inner_sin = tables
    real_spec, imag_spec = spec_pair
    points = outer_cos.shape[0] * inner_cos.shape[0]
    real_inner = jnp.einsum(
        "ckn,mn->ckm", real_spec, inner_cos, precision=PRECISE, preferred_element_type=jnp.float32
    )
    real_inner = real_inner - jnp.einsum(
        "ckn,mn->ckm", imag_spec, inner_sin, precision=PRECISE, preferred_element_type=jnp.float32
    )
    imag_inner = jnp.einsum(
        "ckn,mn->ckm", imag_spec, inner_cos, precision=PRECISE, preferred_element_type=jnp.float32
    )
    imag_inner = imag_inner + jnp.einsum(
        "ckn,mn->ckm", real_spec, inner_sin, precision=PRECISE, preferred_element_type=jnp.float32
    )
    real_turned = real_inner * turn_cos - imag_inner * turn_sin
    imag_turned = imag_inner * turn_cos + real_inner * turn_sin
    result = jnp.einsum(
        "kn,ckm->cnm", outer_cos, real_turned, precision=PRECISE, preferred_element_type=jnp.float32
    )
    result = result - jnp.einsum(
        "kn,ckm->cnm", outer_sin, imag_turned, precision=PRECISE, preferred_element_type=jnp.float32
    )
    return result.reshape(result.shape[0], -1) / points


def product(left_pair, right_pair):
    return (
        left_pair[0] * right_pair[0] - left_pair[1] * right_pair[1],
        left_pair[0] * right_pair[1] + left_pair[1] * right_pair[0],
    )


def product_conj(left_pair, right_pair):
    return (
        left_pair[0] * right_pair[0] + left_pair[1] * right_pair[1],
        left_pair[1] * right_pair[0] - left_pair[0] * right_pair[1],
    )


def forward_inputs(key_rows, value_rows, taps_rows):
    return (
        lax.all_to_all(key_rows, ("ctx", "ch"), split_axis=0, concat_axis=1, tiled=True),
        lax.all_to_all(value_rows, ("ctx", "ch"), split_axis=0, concat_axis=1, tiled=True),
        lax.all_to_all(taps_rows, ("ctx", "ch"), split_axis=0, concat_axis=1, tiled=True),
    )


def backward_inputs(query_rows, grad_rows):
    return (
        lax.all_to_all(query_rows, ("ctx", "ch"), split_axis=0, concat_axis=1, tiled=True),
        lax.all_to_all(grad_rows, ("ctx", "ch"), split_axis=0, concat_axis=1, tiled=True),
    )


def first_outputs(mixed, q_grad):
    moved = (
        lax.all_to_all(mixed, ("ctx", "ch"), split_axis=1, concat_axis=0, tiled=True),
        lax.all_to_all(q_grad, ("ctx", "ch"), split_axis=1, concat_axis=0, tiled=True),
    )
    return tuple((piece.T for piece in moved))


def second_outputs(k_grad, v_grad, filter_grad):
    moved = (
        lax.all_to_all(k_grad, ("ctx", "ch"), split_axis=1, concat_axis=0, tiled=True),
        lax.all_to_all(v_grad, ("ctx", "ch"), split_axis=1, concat_axis=0, tiled=True),
        lax.all_to_all(filter_grad, ("ctx", "ch"), split_axis=1, concat_axis=0, tiled=True),
    )
    return tuple((piece.T for piece in moved))


def general_body(q_proj, k_proj, v_proj, filter_taps, out_grad):
    key_part, value_part, taps_part = forward_inputs(k_proj.T, v_proj.T, filter_taps.T)
    length = key_part.shape[1]
    points = 2 * length
    second = math.gcd(points, 128)
    first = points // second
    tables = build_tables(first, second)
    norm_scale = 1.0 / math.sqrt(length)
    key_wide = key_part.astype(jnp.float32)
    value_wide = value_part.astype(jnp.float32)
    gated = (key_wide * value_wide).astype(jnp.bfloat16)
    gated_spec = forward_spectrum(tables, gated)
    taps_spec = forward_spectrum(tables, taps_part)
    query_part, cotangent = backward_inputs(q_proj.T, out_grad.T)
    query_wide = query_part.astype(jnp.float32)
    grad_wide = cotangent.astype(jnp.float32)
    conv_out = inverse_signal(tables, product(taps_spec, gated_spec)) * norm_scale
    mixed = (query_wide * conv_out).astype(jnp.bfloat16)
    q_grad = (grad_wide * conv_out).astype(jnp.bfloat16)
    mixed, q_grad = first_outputs(mixed, q_grad)
    back_in = (grad_wide * query_wide).astype(jnp.bfloat16)
    back_spec = forward_spectrum(tables, back_in)
    conv_grad = inverse_signal(tables, product_conj(back_spec, taps_spec)) * norm_scale
    filter_grad = (inverse_signal(tables, product_conj(back_spec, gated_spec)) * norm_scale).astype(
        jnp.bfloat16
    )
    k_grad = (conv_grad * value_wide).astype(jnp.bfloat16)
    v_grad = (conv_grad * key_wide).astype(jnp.bfloat16)
    k_grad, v_grad, filter_grad = second_outputs(k_grad, v_grad, filter_grad)
    return (mixed, q_grad, k_grad, v_grad, filter_grad)


MESH_ID = pl.DeviceIdType.MESH
GROUP = 16
VMEM_MIB = 57
BF16 = jnp.bfloat16


def dft_tables(blocks, rows, norm_scale):
    first = 2 * blocks
    points = first * rows
    half = rows // 2
    n1 = np.arange(first)
    outer = np.zeros((first, first))
    outer[0] = 1.0
    outer[1] = np.cos(np.pi * n1)
    for k in range(1, blocks):
        angle = 2.0 * np.pi * (n1 * k % first) / first
        outer[2 * k] = np.cos(angle)
        outer[2 * k + 1] = -np.sin(angle)
    outer_inv = np.linalg.inv(outer)[:blocks] * norm_scale
    outer = outer[:, :blocks]
    n2 = np.arange(rows)
    inner = np.zeros((blocks, 2 * rows, 2 * rows))
    for k in range(1, blocks):
        freq = k + first * np.arange(rows)
        angle = 2.0 * np.pi * (freq[:, None] * n2[None, :] % points) / points
        cos, sin = np.cos(angle), np.sin(angle)
        inner[k] = np.block([[cos, sin], [-sin, cos]])
    for part, k in enumerate((0, blocks)):
        freq = k + first * np.arange(half)
        angle = 2.0 * np.pi * (freq[:, None] * n2[None, :] % points) / points
        columns = slice(part * rows, (part + 1) * rows)
        inner[0, part * half : (part + 1) * half, columns] = np.cos(angle)
        inner[0, rows + part * half : rows + (part + 1) * half, columns] = -np.sin(angle)
    inner[0, rows, :rows] = np.cos(np.pi * n2)
    inner_inv = np.linalg.inv(inner)
    eye = np.eye(GROUP)
    return tuple(
        np.asarray(table, np.float32).astype(BF16)
        for table in (np.kron(outer, eye), inner, inner_inv, np.kron(outer_inv, eye))
    )


def conv_kernel(
    blocks,
    inner_size,
    taps_ref,
    key_ref,
    value_ref,
    query_ref,
    grad_ref,
    outer_hbm,
    inner_hbm,
    inner_inv_hbm,
    outer_inv_hbm,
    mixed_ref,
    qgrad_ref,
    kgrad_ref,
    vgrad_ref,
    fgrad_ref,
    rx,
    tx,
    mid,
    prod,
    taps_spec,
    gated_spec,
    back_spec,
    key_v,
    value_v,
    query_v,
    grad_v,
    gated_v,
    back_v,
    conv_v,
    cgrad_v,
    outer_t,
    inner_t,
    inner_inv_t,
    outer_inv_t,
    table_sem,
    load_sem,
    store_sem,
    send_sem,
    recv_sem,
):
    rows = taps_ref.shape[0]
    lanes = rx.shape[-1]
    me = lax.axis_index("ctx") * inner_size + lax.axis_index("ch")
    sources = (taps_ref, gated_v, back_v)
    loads = ((key_ref, key_v), (value_ref, value_v), (query_ref, query_v), (grad_ref, grad_v))
    results = (conv_v, cgrad_v, fgrad_ref)
    tables = (
        (outer_hbm, outer_t),
        (inner_hbm, inner_t),
        (inner_inv_hbm, inner_inv_t),
        (outer_inv_hbm, outer_inv_t),
    )

    def peer_at(step):
        peer = lax.rem(me + step, blocks)
        return peer, (peer // inner_size, lax.rem(peer, inner_size))

    def row_block(index):
        return pl.ds(pl.multiple_of(index * rows, rows), rows)

    def lane_block(index):
        return pl.ds(pl.multiple_of(index * lanes, lanes), lanes)

    def send_in(which):
        pltpu.make_async_copy(
            sources[which].at[:, lane_block(me)], rx.at[which, row_block(me)], recv_sem.at[which]
        ).start()

        @pl.loop(1, blocks)
        def _(step):
            peer, where = peer_at(step)
            pltpu.make_async_remote_copy(
                src_ref=sources[which].at[:, lane_block(peer)],
                dst_ref=rx.at[which, row_block(me)],
                send_sem=send_sem.at[which],
                recv_sem=recv_sem.at[which],
                device_id=where,
                device_id_type=MESH_ID,
            ).start()

    def send_out(which):
        slot = 3 + which
        pltpu.make_async_copy(
            tx.at[which, row_block(me)], results[which].at[:, lane_block(me)], recv_sem.at[slot]
        ).start()

        @pl.loop(1, blocks)
        def _(step):
            peer, where = peer_at(step)
            pltpu.make_async_remote_copy(
                src_ref=tx.at[which, row_block(peer)],
                dst_ref=results[which].at[:, lane_block(me)],
                send_sem=send_sem.at[slot],
                recv_sem=recv_sem.at[slot],
                device_id=where,
                device_id_type=MESH_ID,
            ).start()

    def wait_in(which):
        pltpu.make_async_copy(rx.at[which], rx.at[which], recv_sem.at[which]).wait()

    def wait_out(which):
        pltpu.make_async_copy(results[which], results[which], recv_sem.at[3 + which]).wait()

    def wait_sent(slot):
        part = rx.at[0, pl.ds(0, (blocks - 1) * rows)]
        pltpu.make_async_copy(part, part, send_sem.at[slot]).wait()

    barrier = pltpu.get_barrier_semaphore()

    @pl.loop(1, blocks)
    def _(step):
        _, where = peer_at(step)
        pl.semaphore_signal(barrier, inc=1, device_id=where, device_id_type=MESH_ID)

    for index, (source, target) in enumerate(loads):
        pltpu.make_async_copy(source, target, load_sem.at[index]).start()

    pl.semaphore_wait(barrier, blocks - 1)

    send_in(0)

    def gate(first, second, target):
        for index in (first, second):
            pltpu.make_async_copy(*loads[index], load_sem.at[index]).wait()

        @pl.loop(0, rows // GROUP)
        def _(group):
            part = pl.ds(pl.multiple_of(group * GROUP, GROUP), GROUP)
            left = loads[first][1][part, :].astype(jnp.float32)
            right = loads[second][1][part, :].astype(jnp.float32)
            target[part, :] = (left * right).astype(BF16)

    gate(0, 1, gated_v)
    send_in(1)
    gate(2, 3, back_v)
    send_in(2)

    for index, (source, target) in enumerate(tables):
        pltpu.make_async_copy(source, target, table_sem.at[index]).start()
    for index, (source, target) in enumerate(tables):
        pltpu.make_async_copy(source, target, table_sem.at[index]).wait()

    pairs = rows // (2 * GROUP)

    def outer_stage(which):
        signal = rx.at[which].reshape(blocks, rows, lanes)

        @pl.loop(0, pairs)
        def _(pair):
            low = pl.ds(pl.multiple_of(pair * 2 * GROUP, GROUP), GROUP)
            high = pl.ds(pl.multiple_of(pair * 2 * GROUP + GROUP, GROUP), GROUP)
            data = jnp.concatenate(
                [
                    signal[:, low, :].reshape(blocks * GROUP, lanes),
                    signal[:, high, :].reshape(blocks * GROUP, lanes),
                ],
                axis=1,
            )
            out = jnp.dot(outer_t[...], data, preferred_element_type=jnp.float32).astype(BF16)
            mid[:, low, :] = out[:, :lanes].reshape(2 * blocks, GROUP, lanes)
            mid[:, high, :] = out[:, lanes:].reshape(2 * blocks, GROUP, lanes)

    def spectrum(k):
        data = mid[pl.ds(2 * k, 2)].reshape(2 * rows, lanes)
        return jnp.dot(inner_t[k], data, preferred_element_type=jnp.float32)

    def real_row(k):
        row = lax.broadcasted_iota(jnp.int32, (rows, lanes), 0)
        return jnp.logical_and(row == 0, k == 0)

    def multiply(left, right, alone):
        lr, li = left[:rows], left[rows:]
        rr, ri = right[:rows], right[rows:]
        real, cross = lr * rr, li * ri
        return jnp.concatenate(
            [jnp.where(alone, real, real - cross), jnp.where(alone, cross, lr * ri + li * rr)], axis=0
        ).astype(BF16)

    def multiply_conj(left, right, alone):
        lr, li = left[:rows], left[rows:]
        rr, ri = right[:rows], right[rows:]
        real, cross = lr * rr, li * ri
        return jnp.concatenate(
            [jnp.where(alone, real, real + cross), jnp.where(alone, cross, li * rr - lr * ri)], axis=0
        ).astype(BF16)

    def inverse_outer(which):
        signal = tx.at[which].reshape(blocks, rows, lanes)

        @pl.loop(0, pairs)
        def _(pair):
            low = pl.ds(pl.multiple_of(pair * 2 * GROUP, GROUP), GROUP)
            high = pl.ds(pl.multiple_of(pair * 2 * GROUP + GROUP, GROUP), GROUP)
            data = jnp.concatenate(
                [
                    prod[:, low, :].reshape(2 * blocks * GROUP, lanes),
                    prod[:, high, :].reshape(2 * blocks * GROUP, lanes),
                ],
                axis=1,
            )
            out = jnp.dot(outer_inv_t[...], data, preferred_element_type=jnp.float32).astype(BF16)
            signal[:, low, :] = out[:, :lanes].reshape(blocks, GROUP, lanes)
            signal[:, high, :] = out[:, lanes:].reshape(blocks, GROUP, lanes)

    def invert(k, pair):
        out = jnp.dot(inner_inv_t[k], pair, preferred_element_type=jnp.float32)
        prod[pl.ds(2 * k, 2)] = out.astype(BF16).reshape(2, rows, lanes)

    wait_in(0)
    outer_stage(0)

    @pl.loop(0, blocks, unroll=2)
    def _(k):
        taps_spec[k] = spectrum(k)

    wait_in(1)
    outer_stage(1)

    @pl.loop(0, blocks, unroll=2)
    def _(k):
        spec = spectrum(k)
        gated_spec[k] = spec
        invert(k, multiply(taps_spec[k], spec, real_row(k)))

    inverse_outer(0)
    send_out(0)

    wait_in(2)
    outer_stage(2)

    @pl.loop(0, blocks, unroll=2)
    def _(k):
        spec = spectrum(k)
        back_spec[k] = spec
        invert(k, multiply_conj(spec, taps_spec[k], real_row(k)))

    inverse_outer(1)
    send_out(1)

    @pl.loop(0, blocks, unroll=2)
    def _(k):
        invert(k, multiply_conj(back_spec[k], gated_spec[k], real_row(k)))

    inverse_outer(2)
    send_out(2)

    def products(which, first, second):
        wait_out(which)
        source = results[which]

        @pl.loop(0, rows // GROUP)
        def _(group):
            part = pl.ds(pl.multiple_of(group * GROUP, GROUP), GROUP)
            conv = source[part, :].astype(jnp.float32)
            for buffer, _, _ in (first, second):
                buffer[part, :] = (buffer[part, :].astype(jnp.float32) * conv).astype(BF16)

        for buffer, target, index in (first, second):
            pltpu.make_async_copy(buffer, target, store_sem.at[index]).start()

    stores = (
        (query_v, mixed_ref, 0),
        (grad_v, qgrad_ref, 1),
        (value_v, kgrad_ref, 2),
        (key_v, vgrad_ref, 3),
    )
    products(0, stores[0], stores[1])
    products(1, stores[2], stores[3])

    for slot in range(6):
        wait_sent(slot)
    for buffer, target, index in stores:
        pltpu.make_async_copy(buffer, target, store_sem.at[index]).wait()
    wait_out(2)


def place_kernel(parts, *refs):
    count = (len(refs) - 3) // 2
    sources, targets = refs[:count], refs[count : 2 * count]
    staged, load_sem, store_sem = refs[2 * count :]
    size = sources[0].shape[0] // parts
    loads, stores = [], []
    for which in range(count):
        for part in range(parts):
            chunk = pl.ds(part * size, size)
            index = which * parts + part
            here = staged.at[which, chunk]
            loads.append(pltpu.make_async_copy(sources[which].at[chunk], here, load_sem.at[index]))
            stores.append(pltpu.make_async_copy(here, targets[which].at[chunk], store_sem.at[index]))
    for load in loads:
        load.start()
    for load, store in zip(loads, stores):
        load.wait()
        store.start()
    for store in stores:
        store.wait()


def place(results):
    anywhere = pl.BlockSpec(memory_space=pl.ANY)
    count, parts = len(results), 4
    rows, channels = results[0].shape
    return pl.pallas_call(
        functools.partial(place_kernel, parts),
        out_shape=tuple(jax.ShapeDtypeStruct(result.shape, result.dtype) for result in results),
        in_specs=[anywhere] * count,
        out_specs=(anywhere,) * count,
        scratch_shapes=[
            pltpu.VMEM((count, rows, channels), BF16),
            pltpu.SemaphoreType.DMA((count * parts,)),
            pltpu.SemaphoreType.DMA((count * parts,)),
        ],
        compiler_params=pltpu.CompilerParams(vmem_limit_bytes=VMEM_MIB * 1024 * 1024),
    )(*results)


def convolve(taps, key, value, query, grad, blocks, inner_size):
    rows, channels = taps.shape
    lanes = channels // blocks
    norm_scale = 1.0 / math.sqrt(rows * blocks)
    tables = dft_tables(blocks, rows, norm_scale)
    signal = jax.ShapeDtypeStruct((rows, channels), BF16)
    anywhere = pl.BlockSpec(memory_space=pl.ANY)
    flops = 2 * lanes * 2 * rows * blocks * (9 * 2 * rows + 6 * blocks * GROUP)
    return pl.pallas_call(
        functools.partial(conv_kernel, blocks, inner_size),
        out_shape=(signal,) * 5,
        in_specs=[pl.BlockSpec(memory_space=pltpu.HBM)] * 9,
        out_specs=(anywhere,) * 5,
        scratch_shapes=[
            pltpu.VMEM((3, blocks * rows, lanes), BF16),
            pltpu.VMEM((3, blocks * rows, lanes), BF16),
            pltpu.VMEM((2 * blocks, rows, lanes), BF16),
            pltpu.VMEM((2 * blocks, rows, lanes), BF16),
            pltpu.VMEM((blocks, 2 * rows, lanes), jnp.float32),
            pltpu.VMEM((blocks, 2 * rows, lanes), jnp.float32),
            pltpu.VMEM((blocks, 2 * rows, lanes), jnp.float32),
        ]
        + [pltpu.VMEM((rows, channels), BF16)] * 8
        + [pltpu.VMEM(table.shape, BF16) for table in tables]
        + [
            pltpu.SemaphoreType.DMA((4,)),
            pltpu.SemaphoreType.DMA((4,)),
            pltpu.SemaphoreType.DMA((4,)),
            pltpu.SemaphoreType.DMA((6,)),
            pltpu.SemaphoreType.DMA((6,)),
        ],
        compiler_params=pltpu.CompilerParams(
            collective_id=0, has_side_effects=True, vmem_limit_bytes=VMEM_MIB * 1024 * 1024
        ),
        cost_estimate=pl.CostEstimate(flops=flops, bytes_accessed=32 * rows * channels, transcendentals=0),
    )(taps, key, value, query, grad, *(jnp.asarray(table) for table in tables))


def fast_body(blocks, inner_size, q_proj, k_proj, v_proj, filter_taps, out_grad):
    return place(convolve(filter_taps, k_proj, v_proj, q_proj, out_grad, blocks, inner_size))


def solution(mesh):
    blocks = mesh.shape["ctx"] * mesh.shape["ch"]
    inner_size = mesh.shape["ch"]
    spec = P(("ctx", "ch"), None)

    def run(*arrays):
        tokens, channels = arrays[0].shape
        if channels == 128 * blocks and tokens == 128 * blocks:
            body = functools.partial(fast_body, blocks, inner_size)
        else:
            body = general_body
        return jax.shard_map(
            body, mesh=mesh, in_specs=(spec,) * 5, out_specs=(spec,) * 5, check_vma=False
        )(*arrays)

    return run
```
